32 devices in a mesh: samp: 4 (over y, x), pre: 8 (over z, core).
Axes of the slice: x: 2, y: 2, z: 4, core: 2. Of those that a mesh axis runs over, the one named last changes fastest.
Arguments:
- queries: bfloat16 [64, 32, 128], P(('samp', 'pre')), may hold values from -15 to 15
- prefix_keys: bfloat16 [4, 6144, 128], P(None, ('pre', 'samp')), may hold values from -6 to 6
- prefix_values: bfloat16 [4, 6144, 128], P(None, ('pre', 'samp')), may hold values from -6 to 6
- suffix_keys: bfloat16 [64, 4, 128, 128], P(('samp', 'pre')), may hold values from -8 to 8
- suffix_values: bfloat16 [64, 4, 128, 128], P(('samp', 'pre')), may hold values from -6 to 6
- suffix_lengths: int32 [64], P(('samp', 'pre')), may hold values from 2 to 128, as said below
- prompt_length: int32 [1], replicated, may hold values from 3072 to 6144
- out_weight: bfloat16 [4096, 5120], P('pre'), may hold values from -0.09375 to 0.09375
Outputs:
- mixed: bfloat16 [64, 5120], P(('samp', 'pre'))
The draws below stay inside these ranges and needn't reach their ends.
Inputs may be any that keep to these rules, and one draw needn't show every extreme that they name: `suffix_lengths`: some sample fills all 128 slots.
All inputs are finite; a program needn't handle non-finite values.
Results may differ from the reference program's by a relative error of at most 0.013.
Values may be sent and summed in bfloat16 or wider, within the bound.
A program may use at most 64 MiB of HBM per device.

```python
import math
import jax
import jax.numpy as jnp
from jax import lax

D = 5120
H = 32
KVH = 4
HD = 128
P_DEV = 768
SUF = 128
SAMPLES = 64
PREFIX = 6144
N_PRE = 8


def draw_queries(key, part):
    key = jax.random.fold_in(key, 5)
    base = jnp.clip(2.5 * jax.random.normal(key, (SAMPLES, H, HD), jnp.float32), -15.0, 15.0)
    return base.astype(jnp.bfloat16)


def draw_prefix_keys(key, part):
    key = jax.random.fold_in(key, 3)
    base = jnp.clip(jax.random.normal(key, (KVH, PREFIX, HD), jnp.float32), -6.0, 6.0)
    return base.astype(jnp.bfloat16)


def draw_suffix_keys(key, part):
    key = jax.random.fold_in(key, 4)
    base = jnp.clip(1.4 * jax.random.normal(key, (SAMPLES, KVH, SUF, HD), jnp.float32), -8.0, 8.0)
    return base.astype(jnp.bfloat16)


def draw_suffix_lengths(key, part):
    key = jax.random.fold_in(key, 7)
    lengths = jax.random.randint(jax.random.fold_in(key, 1), (SAMPLES,), 2, SUF + 1)
    longest = jax.random.randint(jax.random.fold_in(key, 2), (), 0, SAMPLES)
    return jnp.where(jnp.arange(SAMPLES) == longest, SUF, lengths).astype(jnp.int32)


def block_scale(key, extent, split, least, largest):
    def one(axis_at, shards_of):
        steps = jax.random.uniform(jax.random.fold_in(jax.random.fold_in(key, 6), axis_at), (shards_of,), jnp.float32, least / len(split), largest / len(split))
        return jnp.repeat(jnp.exp(steps), extent[axis_at] // shards_of).reshape((-1,) + (1,) * (len(extent) - axis_at - 1))

    loudness = one(*split[0])
    for cut in split[1:]:
        loudness = loudness * one(*cut)
    return loudness


def centred(stream_key, extent, scale, most, pieces=(), kind=jnp.bfloat16):
    entries = scale * jax.random.normal(stream_key, extent, jnp.float32)
    if pieces:
        entries = entries * block_scale(stream_key, extent, pieces, -0.22, 0.18)
    return jnp.clip(entries, -most, most).astype(kind)


def setup_inputs(seed: int = 0) -> dict:
    streams_of = jax.random.split(jax.random.key(seed), 9)
    return {
        "queries": draw_queries(jax.random.fold_in(streams_of[8], 71), 0),
        "prefix_keys": draw_prefix_keys(jax.random.fold_in(streams_of[8], 71), 0),
        "prefix_values": centred(streams_of[2], (KVH, PREFIX, HD), 1.0, 6.0, ((1, 32),)),
        "suffix_keys": draw_suffix_keys(jax.random.fold_in(streams_of[8], 71), 0),
        "suffix_values": centred(streams_of[4], (SAMPLES, KVH, SUF, HD), 1.0, 6.0, ((0, 32),)),
        "suffix_lengths": draw_suffix_lengths(jax.random.fold_in(streams_of[8], 71), 0),
        "prompt_length": jax.random.randint(streams_of[6], (1,), PREFIX // 2, PREFIX + 1).astype(jnp.int32),
        "out_weight": centred(streams_of[7], (H * HD, D), (H * HD) ** -0.5, 0.09375, ((0, 8),)),
    }


NEGATIVE = -1e+30

def partial_softmax(grouped, keys, values, visible, score_form, value_form):
    scaling = 1.0 / math.sqrt(HD)
    scores = jnp.einsum(score_form, grouped, keys.astype(jnp.float32)) * scaling
    scores = jnp.where(visible, scores, NEGATIVE)
    peaks = lax.optimization_barrier(jnp.max(scores, axis=-1))
    weights = jnp.where(visible, jnp.exp(scores - peaks[..., None]), 0.0)
    totals = lax.optimization_barrier(jnp.sum(weights, axis=-1))
    rounded = lax.optimization_barrier(weights.astype(jnp.bfloat16)).astype(jnp.float32)
    results = jnp.einsum(value_form, rounded, values.astype(jnp.float32)).astype(jnp.bfloat16)
    return (results, peaks, totals)

def absorb(state, parts):
    peaks, totals, numerator = state
    results, new_peaks, new_totals = parts
    joined = jnp.maximum(peaks, new_peaks)
    old_weight = jnp.exp(peaks - joined)
    new_weight = jnp.exp(new_peaks - joined)
    widened = lax.optimization_barrier(results).astype(jnp.float32)
    return (joined, old_weight * totals + new_weight * new_totals, old_weight[..., None] * numerator + new_weight[..., None] * widened)

def reference(queries, prefix_keys, prefix_values, suffix_keys, suffix_values, suffix_lengths, prompt_length, out_weight):
    samples = queries.shape[0]
    ratio = H // KVH
    grouped = queries.reshape(samples, KVH, ratio, HD).astype(jnp.float32)
    key_blocks = prefix_keys.reshape(KVH, N_PRE, P_DEV, HD).transpose(1, 0, 2, 3)
    value_blocks = prefix_values.reshape(KVH, N_PRE, P_DEV, HD).transpose(1, 0, 2, 3)
    starts = jnp.arange(N_PRE, dtype=jnp.int32) * P_DEV
    state = (jnp.full((samples, KVH, ratio), NEGATIVE, jnp.float32), jnp.zeros((samples, KVH, ratio), jnp.float32), jnp.zeros((samples, KVH, ratio, HD), jnp.float32))

    def block_step(carry, operands):
        block_keys, block_values, begin = operands
        visible = begin + jnp.arange(P_DEV, dtype=jnp.int32) < prompt_length[0]
        parts = partial_softmax(grouped, block_keys, block_values, visible, 'sgjd,gpd->sgjp', 'sgjp,gpd->sgjd')
        return (absorb(carry, parts), jnp.zeros((), jnp.float32))
    state, unused = lax.scan(block_step, state, (key_blocks, value_blocks, starts))
    visible = (jnp.arange(SUF, dtype=jnp.int32)[None, :] < suffix_lengths[:, None])[:, None, None, :]
    parts = partial_softmax(grouped, suffix_keys, suffix_values, visible, 'sgjd,sgpd->sgjp', 'sgjp,sgpd->sgjd')
    peaks, totals, numerator = absorb(state, parts)
    attention = (numerator / totals[..., None]).astype(jnp.bfloat16).reshape(samples, H * HD)
    block_rows = H * HD // N_PRE
    feature_blocks = attention.reshape(samples, N_PRE, block_rows).transpose(1, 0, 2)
    weight_blocks = out_weight.reshape(N_PRE, block_rows, out_weight.shape[1])

    def head_step(total, operands):
        features, weights = operands
        term = jnp.dot(features, weights, preferred_element_type=jnp.float32)
        term = lax.optimization_barrier(term.astype(jnp.bfloat16)).astype(jnp.float32)
        return (total + term, jnp.zeros((), jnp.float32))
    summed, unused = lax.scan(head_step, jnp.zeros((samples, out_weight.shape[1]), jnp.float32), (feature_blocks, weight_blocks))
    return summed.astype(jnp.bfloat16)
```

```python
import functools
import math

import jax
import jax.numpy as jnp
from jax import lax
from jax.experimental import pallas as pl
from jax.experimental.pallas import tpu as pltpu
from jax.sharding import PartitionSpec as P

NEGATIVE = -1e30


def prompt_partial(grouped, block_keys, block_values, visible):
    scaling = 1.0 / math.sqrt(grouped.shape[-1])
    by_head = jnp.transpose(grouped, (1, 0, 2, 3))

    def one_head(operands):
        head_queries, head_keys, head_values = operands
        scores = (
            lax.dot_general(
                head_queries,
                head_keys,
                (((2,), (1,)), ((), ())),
                preferred_element_type=jnp.float32,
            )
            * scaling
        )
        scores = jnp.where(visible, scores, NEGATIVE)
        peaks = jnp.max(scores, axis=-1)
        weights = jnp.where(visible, jnp.exp(scores - peaks[..., None]), 0.0)
        totals = jnp.sum(weights, axis=-1)
        results = lax.dot_general(
            weights.astype(jnp.bfloat16),
            head_values,
            (((2,), (0,)), ((), ())),
            preferred_element_type=jnp.float32,
        )
        return (results.astype(jnp.bfloat16), peaks, totals)

    results, peaks, totals = lax.map(one_head, (by_head, block_keys, block_values))
    count = grouped.shape[0]
    heads = grouped.shape[1] * grouped.shape[2]
    results = jnp.transpose(results, (1, 0, 2, 3)).reshape(count, heads, grouped.shape[3])
    peaks = jnp.transpose(peaks, (1, 0, 2)).reshape(count, heads)
    totals = jnp.transpose(totals, (1, 0, 2)).reshape(count, heads)
    return (results, peaks, totals)


def suffix_partial(grouped, suffix_keys, suffix_values, suffix_lengths):
    scaling = 1.0 / math.sqrt(grouped.shape[-1])
    slots = suffix_keys.shape[2]
    visible = (jnp.arange(slots, dtype=jnp.int32)[None, :] < suffix_lengths[:, None])[
        :, None, None, :
    ]
    scores = (
        jnp.einsum("sgjd,sgpd->sgjp", grouped, suffix_keys, preferred_element_type=jnp.float32)
        * scaling
    )
    scores = jnp.where(visible, scores, NEGATIVE)
    peaks = jnp.max(scores, axis=-1)
    weights = jnp.where(visible, jnp.exp(scores - peaks[..., None]), 0.0)
    totals = jnp.sum(weights, axis=-1)
    results = jnp.einsum(
        "sgjp,sgpd->sgjd",
        weights.astype(jnp.bfloat16),
        suffix_values,
        preferred_element_type=jnp.float32,
    )
    count = grouped.shape[0]
    heads = grouped.shape[1] * grouped.shape[2]
    return (
        results.astype(jnp.bfloat16).reshape(count, heads, grouped.shape[3]),
        peaks.reshape(count, heads),
        totals.reshape(count, heads),
    )


def merge_parts(results, peaks, totals):
    highest = jnp.max(peaks, axis=0)
    weights = jnp.exp(peaks - highest)
    denominator = jnp.sum(weights * totals, axis=0)
    numerator = jnp.sum(weights[..., None] * results.astype(jnp.float32), axis=0)
    return (numerator / denominator[..., None]).astype(jnp.bfloat16)


def shards(
    queries,
    prefix_keys,
    prefix_values,
    suffix_keys,
    suffix_values,
    suffix_lengths,
    prompt_length,
    out_weight,
):
    own_samples = queries.shape[0]
    heads = queries.shape[1]
    head_width = queries.shape[2]
    key_heads = prefix_keys.shape[0]
    ratio = heads // key_heads
    groups = lax.axis_size("pre")
    head_share = heads // groups
    block_keys, block_values = (
        lax.all_gather(prefix_keys, "samp", axis=1, tiled=True),
        lax.all_gather(prefix_values, "samp", axis=1, tiled=True),
    )
    block_length = block_keys.shape[1]
    group_queries = lax.all_gather(queries, "pre", axis=0, tiled=True)
    group_count = group_queries.shape[0]
    positions = lax.axis_index("pre") * block_length + jnp.arange(block_length, dtype=jnp.int32)
    visible = positions < prompt_length[0]
    own_grouped = queries.reshape(own_samples, key_heads, ratio, head_width)
    suffix_results, suffix_peaks, suffix_totals = suffix_partial(
        own_grouped, suffix_keys, suffix_values, suffix_lengths
    )
    group_grouped = group_queries.reshape(group_count, key_heads, ratio, head_width)
    prompt_results, prompt_peaks, prompt_totals = prompt_partial(
        group_grouped, block_keys, block_values, visible
    )
    received_results = lax.all_to_all(
        prompt_results[None], "pre", split_axis=1, concat_axis=0, tiled=True
    )
    received_peaks, received_totals = (
        lax.all_to_all(prompt_peaks[None], "pre", split_axis=1, concat_axis=0, tiled=True),
        lax.all_to_all(prompt_totals[None], "pre", split_axis=1, concat_axis=0, tiled=True),
    )
    attention = merge_parts(
        jnp.concatenate([received_results, suffix_results[None]], 0),
        jnp.concatenate([received_peaks, suffix_peaks[None]], 0),
        jnp.concatenate([received_totals, suffix_totals[None]], 0),
    )
    head_rows = lax.all_to_all(attention, "pre", split_axis=1, concat_axis=0, tiled=True)
    flat_rows = head_rows.reshape(group_count, head_share * head_width)
    return lax.psum_scatter(
        jnp.dot(flat_rows, out_weight, preferred_element_type=jnp.float32).astype(jnp.bfloat16),
        "pre",
        scatter_dimension=0,
        tiled=True,
    )


MESH = pl.DeviceIdType.MESH
LOG2E = 1.4426950408889634
CUTS = 8


def head_of(samp, pre, key_heads):
    return lax.rem(samp + pre // 2 + 2 * lax.rem(pre, 2), key_heads)


def fused_kernel(
    samp,
    pre,
    length_ref,
    prompt_ref,
    q_ref,
    pk_ref,
    pv_ref,
    sk_ref,
    sv_ref,
    w_ref,
    out_ref,
    qf,
    qstage,
    qbuf,
    kvbuf,
    sk,
    sv,
    w,
    sufstage,
    sufbuf,
    ostage,
    obuf,
    sstage,
    sbuf,
    tscr,
    attscr,
    cut,
    rstage,
    rbuf,
    q_send,
    q_recv,
    kv_send,
    kv_recv,
    local_sem,
    suf_send,
    suf_recv,
    o_send,
    o_recv,
    s_send,
    s_recv,
    r_send,
    r_recv,
):
    key_heads = pk_ref.shape[0]
    width = q_ref.shape[2]
    share = pk_ref.shape[1]
    total = samp * pre
    g = lax.axis_index("samp")
    b = lax.axis_index("pre")
    me = g * pre + b
    head = head_of(g, b, key_heads)
    scale = LOG2E / math.sqrt(width)

    def go(source, target, send, recv, to_samp, to_pre):
        pltpu.make_async_remote_copy(
            src_ref=source,
            dst_ref=target,
            send_sem=send,
            recv_sem=recv,
            device_id=(to_samp, to_pre),
            device_id_type=MESH,
        ).start()

    def drain(ref, sem):
        pltpu.make_async_copy(ref, ref, sem).wait()

    barrier = pltpu.get_barrier_semaphore()

    @pl.loop(1, total)
    def _(i):
        t = lax.rem(me + i, total)
        pl.semaphore_signal(
            barrier, inc=1, device_id=(t // pre, lax.rem(t, pre)), device_id_type=MESH
        )

    pltpu.make_async_copy(sk_ref, sk, local_sem.at[0]).start()
    pltpu.make_async_copy(sv_ref, sv, local_sem.at[1]).start()
    pltpu.make_async_copy(pk_ref.at[head], kvbuf.at[g, 0], kv_recv.at[g]).start()
    pltpu.make_async_copy(pv_ref.at[head], kvbuf.at[g, 1], kv_recv.at[g]).start()
    pltpu.make_async_copy(w_ref, w, local_sem.at[2]).start()

    wide = q_ref[...].astype(jnp.float32)
    qf[...] = wide
    for h in range(key_heads):
        for c in range(2):
            for s in range(2):
                row = 16 * h + 8 * c + 4 * s
                tscr[pl.ds(row, 4), :] = qf[s, pl.ds(8 * h + 4 * c, 4), :]
    for h in range(key_heads):
        qstage[h] = tscr[pl.ds(16 * h, 16), :].astype(jnp.bfloat16)

    pltpu.make_async_copy(qstage.at[head], qbuf.at[me], q_recv).start()
    pl.semaphore_wait(barrier, total - 1)

    @pl.loop(1, total)
    def _(i):
        t = lax.rem(me + i, total)
        to_samp, to_pre = t // pre, lax.rem(t, pre)
        go(
            qstage.at[head_of(to_samp, to_pre, key_heads)],
            qbuf.at[me],
            q_send,
            q_recv,
            to_samp,
            to_pre,
        )

    for step in range(1, samp):
        to = lax.rem(g + step, samp)
        his = head_of(to, b, key_heads)
        go(pk_ref.at[his], kvbuf.at[g, 0], kv_send, kv_recv.at[g], to, b)
        go(pv_ref.at[his], kvbuf.at[g, 1], kv_send, kv_recv.at[g], to, b)

    pltpu.make_async_copy(sk_ref, sk, local_sem.at[0]).wait()
    pltpu.make_async_copy(sv_ref, sv, local_sem.at[1]).wait()
    slots = sk.shape[2]
    rows = lax.broadcasted_iota(jnp.int32, (16, 2 * slots), 0)
    cols = lax.broadcasted_iota(jnp.int32, (16, 2 * slots), 1)
    second_row = lax.rem(rows, 8) >= 4
    first_end = jnp.where(second_row, 0, length_ref[0])
    second_end = jnp.where(second_row, length_ref[1], 0) + slots
    seen = cols < jnp.where(cols < slots, first_end, second_end)
    for h in range(key_heads):
        keys = jnp.concatenate([sk[0, h], sk[1, h]], axis=0)
        values = jnp.concatenate([sv[0, h], sv[1, h]], axis=0)
        scores = lax.dot_general(
            qstage[h], keys, (((1,), (1,)), ((), ())), preferred_element_type=jnp.float32
        )
        scores = jnp.where(seen, scores * scale, NEGATIVE)
        peaks = jnp.max(scores, axis=1, keepdims=True)
        weights = jnp.exp2(scores - peaks)
        totals = jnp.sum(weights, axis=1, keepdims=True)
        results = jnp.dot(weights.astype(jnp.bfloat16), values, preferred_element_type=jnp.float32)
        peaks = jnp.broadcast_to(peaks, (16, width))
        totals = jnp.broadcast_to(totals, (16, width))
        for c in range(2):
            sufstage[2 * h + c, 0:8] = results[8 * c : 8 * c + 8]
            sufstage[2 * h + c, 8:16] = peaks[8 * c : 8 * c + 8]
            sufstage[2 * h + c, 16:24] = totals[8 * c : 8 * c + 8]

    pltpu.make_async_copy(sufstage.at[b], sufbuf.at[b], suf_recv).start()

    @pl.loop(1, pre)
    def _(i):
        to = lax.rem(b + i, pre)
        go(sufstage.at[to], sufbuf.at[b], suf_send, suf_recv, g, to)

    drain(qbuf, q_recv)
    queries = qbuf[...].reshape(total * 16, width)
    count = total * 16
    peak = sums = result = None
    for step in range(samp):
        slot = lax.rem(g + step, samp)
        drain(kvbuf.at[slot], kv_recv.at[slot])
        scores = lax.dot_general(
            kvbuf[slot, 0],
            queries,
            (((1,), (1,)), ((), ())),
            preferred_element_type=jnp.float32,
        )
        first = (b * samp + slot) * share
        place = first + lax.broadcasted_iota(jnp.int32, (share, count), 0)
        scores = jnp.where(place < prompt_ref[0], scores * scale, NEGATIVE)
        new_peak = jnp.max(scores, axis=0, keepdims=True)
        if step:
            new_peak = jnp.maximum(new_peak, peak)
        weights = jnp.exp2(scores - new_peak)
        new_sums = jnp.sum(weights, axis=0, keepdims=True)
        new_result = lax.dot_general(
            kvbuf[slot, 1],
            weights.astype(jnp.bfloat16),
            (((0,), (0,)), ((), ())),
            preferred_element_type=jnp.float32,
        )
        if step:
            keep = jnp.exp2(peak - new_peak)
            new_sums = new_sums + keep * sums
            new_result = new_result + keep * result
        peak, sums, result = new_peak, new_sums, new_result

    per = pre * 16
    for t in range(samp):
        block = result[:, per * t : per * (t + 1)].T.reshape(pre, 2, 8, width)
        for c in range(2):
            ostage[t, c] = block[:, c].reshape(pre * 8, width).astype(jnp.bfloat16)
        tile = lax.broadcasted_iota(jnp.int32, (8, per), 0)
        sstage[t] = jnp.where(
            tile == 0, peak[:, per * t : per * (t + 1)], sums[:, per * t : per * (t + 1)]
        )

    slot8 = pl.ds(pl.multiple_of(b * 8, 8), 8)
    for step in range(samp):
        to = lax.rem(g + step, samp)
        for c in range(2):
            k = 2 * head + c

            def here(to=to, c=c):
                pltpu.make_async_copy(ostage.at[to, c], obuf.at[b], o_recv).start()
                pltpu.make_async_copy(sstage.at[to], sbuf.at[slot8], s_recv).start()

            def there(to=to, c=c, k=k):
                go(ostage.at[to, c], obuf.at[b], o_send, o_recv, to, k)
                go(sstage.at[to], sbuf.at[slot8], s_send, s_recv, to, k)

            if step:
                there()
            else:
                pl.when(k == b)(here)
                pl.when(k != b)(there)

    drain(sufbuf, suf_recv)
    suffix = sufbuf[...]
    suffix_result = suffix[:, 0:8].reshape(pre * 8, width)
    suffix_peak = suffix[:, 8:16].reshape(pre * 8, width)
    suffix_total = suffix[:, 16:24].reshape(pre * 8, width)
    drain(sbuf, s_recv)
    peaks = sbuf[pl.ds(0, pre, stride=8), :]
    totals = sbuf[pl.ds(1, pre, stride=8), :]
    top = jnp.max(peaks, axis=0, keepdims=True)
    shares = jnp.exp2(peaks - top)
    bottom = jnp.sum(shares * totals, axis=0, keepdims=True)
    stacked = jnp.concatenate(
        [
            shares,
            jnp.broadcast_to(top, (8, per)),
            jnp.broadcast_to(bottom, (8, per)),
            jnp.zeros((per - 16 - pre, per), jnp.float32),
        ],
        axis=0,
    )
    tscr[...] = stacked.T
    turned = tscr[...].reshape(pre, 2, 8, per)
    turned = jnp.where(lax.rem(b, 2) == 0, turned[:, 0], turned[:, 1]).reshape(pre * 8, per)
    drain(obuf, o_recv)
    prompt_result = jnp.zeros((pre * 8, width), jnp.float32)
    for i in range(pre):
        prompt_result += turned[:, i : i + 1] * obuf[i].astype(jnp.float32)
    prompt_peak = turned[:, pre : pre + 1]
    prompt_total = turned[:, pre + 8 : pre + 9]
    highest = jnp.maximum(prompt_peak, suffix_peak)
    old = jnp.exp2(prompt_peak - highest)
    new = jnp.exp2(suffix_peak - highest)
    attscr[...] = (old * prompt_result + new * suffix_result) / (
        old * prompt_total + new * suffix_total
    )
    attention = jnp.concatenate(
        [attscr[pl.ds(j, 2 * pre, stride=4), :] for j in range(4)], axis=1
    ).astype(jnp.bfloat16)

    pltpu.make_async_copy(w_ref, w, local_sem.at[2]).wait()
    lanes = cut.shape[2]
    piece = cut.shape[0] * lanes
    for p in range(0, CUTS, 2):
        part = jnp.dot(
            attention,
            w[:, p * piece : (p + 2) * piece],
            preferred_element_type=jnp.float32,
        )
        for i in range(2):
            for n in range(cut.shape[0]):
                at = i * piece + n * lanes
                cut[n, pl.ds(p + i, 2 * pre, stride=CUTS), :] = part[:, at : at + lanes]
    for n in range(cut.shape[0]):
        rows = cut[n].reshape(pre, 2 * CUTS, lanes)
        rstage[:, :, n * lanes : (n + 1) * lanes] = rows.astype(jnp.bfloat16)

    pltpu.make_async_copy(rstage.at[b], rbuf.at[b], r_recv).start()

    @pl.loop(1, pre)
    def _(i):
        to = lax.rem(b + i, pre)
        go(rstage.at[to], rbuf.at[b], r_send, r_recv, g, to)

    drain(rbuf, r_recv)
    out_ref[...] = jnp.sum(rbuf[...].astype(jnp.float32), axis=0).astype(jnp.bfloat16)

    drain(qbuf.at[pl.ds(0, total - 1)], q_send)
    drain(kvbuf.at[pl.ds(0, samp - 1)], kv_send)
    drain(sufbuf.at[pl.ds(0, pre - 1)], suf_send)
    drain(rbuf.at[pl.ds(0, pre - 1)], r_send)
    mine = (2 * head == b) | (2 * head + 1 == b)

    @pl.when(mine)
    def _():
        drain(obuf.at[pl.ds(0, pre - 1)], o_send)
        drain(sbuf.at[pl.ds(0, 8 * (pre - 1))], s_send)

    @pl.when(jnp.logical_not(mine))
    def _():
        drain(obuf, o_send)
        drain(sbuf, s_send)


def fused_shards(
    samp,
    pre,
    queries,
    prefix_keys,
    prefix_values,
    suffix_keys,
    suffix_values,
    suffix_lengths,
    prompt_length,
    out_weight,
):
    own, heads, width = queries.shape
    key_heads, share, _ = prefix_keys.shape
    features = out_weight.shape[1]
    piece = features // CUTS
    total = samp * pre
    bf16, f32 = jnp.bfloat16, jnp.float32
    dma = pltpu.SemaphoreType.DMA
    vmem = pl.BlockSpec(memory_space=pltpu.VMEM)
    smem = pl.BlockSpec(memory_space=pltpu.SMEM)
    hbm = pl.BlockSpec(memory_space=pl.ANY)
    out = pl.pallas_call(
        functools.partial(fused_kernel, samp, pre),
        out_shape=jax.ShapeDtypeStruct((own * CUTS, piece), bf16),
        in_specs=[smem, smem, vmem, hbm, hbm, hbm, hbm, hbm],
        out_specs=vmem,
        scratch_shapes=[
            pltpu.VMEM((own, heads, width), f32),
            pltpu.VMEM((key_heads, 16, width), bf16),
            pltpu.VMEM((total, 16, width), bf16),
            pltpu.VMEM((samp, 2, share, width), bf16),
            pltpu.VMEM(suffix_keys.shape, bf16),
            pltpu.VMEM(suffix_values.shape, bf16),
            pltpu.VMEM(out_weight.shape, bf16),
            pltpu.VMEM((pre, 24, width), f32),
            pltpu.VMEM((pre, 24, width), f32),
            pltpu.VMEM((samp, 2, pre * 8, width), bf16),
            pltpu.VMEM((pre, pre * 8, width), bf16),
            pltpu.VMEM((samp, 8, pre * 16), f32),
            pltpu.VMEM((pre * 8, pre * 16), f32),
            pltpu.VMEM((pre * 16, width), f32),
            pltpu.VMEM((pre * 8, width), f32),
            pltpu.VMEM((piece // 128, own * pre * CUTS, 128), f32),
            pltpu.VMEM((pre, own * CUTS, piece), bf16),
            pltpu.VMEM((pre, own * CUTS, piece), bf16),
            dma,
            dma,
            dma,
            dma((samp,)),
            dma((3,)),
            dma,
            dma,
            dma,
            dma,
            dma,
            dma,
            dma,
            dma,
        ],
        compiler_params=pltpu.CompilerParams(
            collective_id=0, has_side_effects=True, vmem_limit_bytes=40 * 1024 * 1024
        ),
        cost_estimate=pl.CostEstimate(
            flops=300_000_000, bytes_accessed=7_000_000, transcendentals=400_000
        ),
    )(
        suffix_lengths,
        prompt_length,
        queries,
        prefix_keys,
        prefix_values,
        suffix_keys,
        suffix_values,
        out_weight,
    )
    return out.reshape(own, features)


def solution(mesh):
    samp, pre = mesh.shape["samp"], mesh.shape["pre"]

    def body(queries, prefix_keys, *rest):
        own, heads, width = queries.shape
        key_heads = prefix_keys.shape[0]
        fits = (
            samp == key_heads
            and pre == 2 * key_heads
            and heads == 8 * key_heads
            and own == 2
            and pre * 16 == width
        )
        if fits:
            return fused_shards(samp, pre, queries, prefix_keys, *rest)
        return shards(queries, prefix_keys, *rest)

    return jax.shard_map(
        body,
        mesh=mesh,
        in_specs=(
            P(("samp", "pre"), None, None),
            P(None, ("pre", "samp"), None),
            P(None, ("pre", "samp"), None),
            P(("samp", "pre"), None, None, None),
            P(("samp", "pre"), None, None, None),
            P(("samp", "pre")),
            P(),
            P("pre", None),
        ),
        out_specs=P(("samp", "pre"), None),
        check_vma=False,
    )
```

```python
import functools
import math

import jax
import jax.numpy as jnp
from jax import lax
from jax.experimental import pallas as pl
from jax.experimental.pallas import tpu as pltpu
from jax.sharding import PartitionSpec as P

NEGATIVE = -1e30


def prompt_partial(grouped, block_keys, block_values, visible):
    scaling = 1.0 / math.sqrt(grouped.shape[-1])
    by_head = jnp.transpose(grouped, (1, 0, 2, 3))

    def one_head(operands):
        head_queries, head_keys, head_values = operands
        scores = (
            lax.dot_general(
                head_queries,
                head_keys,
                (((2,), (1,)), ((), ())),
                preferred_element_type=jnp.float32,
            )
            * scaling
        )
        scores = jnp.where(visible, scores, NEGATIVE)
        peaks = jnp.max(scores, axis=-1)
        weights = jnp.where(visible, jnp.exp(scores - peaks[..., None]), 0.0)
        totals = jnp.sum(weights, axis=-1)
        results = lax.dot_general(
            weights.astype(jnp.bfloat16),
            head_values,
            (((2,), (0,)), ((), ())),
            preferred_element_type=jnp.float32,
        )
        return (results.astype(jnp.bfloat16), peaks, totals)

    results, peaks, totals = lax.map(one_head, (by_head, block_keys, block_values))
    count = grouped.shape[0]
    heads = grouped.shape[1] * grouped.shape[2]
    results = jnp.transpose(results, (1, 0, 2, 3)).reshape(count, heads, grouped.shape[3])
    peaks = jnp.transpose(peaks, (1, 0, 2)).reshape(count, heads)
    totals = jnp.transpose(totals, (1, 0, 2)).reshape(count, heads)
    return (results, peaks, totals)


def suffix_partial(grouped, suffix_keys, suffix_values, suffix_lengths):
    scaling = 1.0 / math.sqrt(grouped.shape[-1])
    slots = suffix_keys.shape[2]
    visible = (jnp.arange(slots, dtype=jnp.int32)[None, :] < suffix_lengths[:, None])[
        :, None, None, :
    ]
    scores = (
        jnp.einsum("sgjd,sgpd->sgjp", grouped, suffix_keys, preferred_element_type=jnp.float32)
        * scaling
    )
    scores = jnp.where(visible, scores, NEGATIVE)
    peaks = jnp.max(scores, axis=-1)
    weights = jnp.where(visible, jnp.exp(scores - peaks[..., None]), 0.0)
    totals = jnp.sum(weights, axis=-1)
    results = jnp.einsum(
        "sgjp,sgpd->sgjd",
        weights.astype(jnp.bfloat16),
        suffix_values,
        preferred_element_type=jnp.float32,
    )
    count = grouped.shape[0]
    heads = grouped.shape[1] * grouped.shape[2]
    return (
        results.astype(jnp.bfloat16).reshape(count, heads, grouped.shape[3]),
        peaks.reshape(count, heads),
        totals.reshape(count, heads),
    )


def merge_parts(results, peaks, totals):
    highest = jnp.max(peaks, axis=0)
    weights = jnp.exp(peaks - highest)
    denominator = jnp.sum(weights * totals, axis=0)
    numerator = jnp.sum(weights[..., None] * results.astype(jnp.float32), axis=0)
    return (numerator / denominator[..., None]).astype(jnp.bfloat16)


def shards(
    queries,
    prefix_keys,
    prefix_values,
    suffix_keys,
    suffix_values,
    suffix_lengths,
    prompt_length,
    out_weight,
):
    own_samples = queries.shape[0]
    heads = queries.shape[1]
    head_width = queries.shape[2]
    key_heads = prefix_keys.shape[0]
    ratio = heads // key_heads
    groups = lax.axis_size("pre")
    head_share = heads // groups
    block_keys, block_values = (
        lax.all_gather(prefix_keys, "samp", axis=1, tiled=True),
        lax.all_gather(prefix_values, "samp", axis=1, tiled=True),
    )
    block_length = block_keys.shape[1]
    group_queries = lax.all_gather(queries, "pre", axis=0, tiled=True)
    group_count = group_queries.shape[0]
    positions = lax.axis_index("pre") * block_length + jnp.arange(block_length, dtype=jnp.int32)
    visible = positions < prompt_length[0]
    own_grouped = queries.reshape(own_samples, key_heads, ratio, head_width)
    suffix_results, suffix_peaks, suffix_totals = suffix_partial(
        own_grouped, suffix_keys, suffix_values, suffix_lengths
    )
    group_grouped = group_queries.reshape(group_count, key_heads, ratio, head_width)
    prompt_results, prompt_peaks, prompt_totals = prompt_partial(
        group_grouped, block_keys, block_values, visible
    )
    received_results = lax.all_to_all(
        prompt_results[None], "pre", split_axis=1, concat_axis=0, tiled=True
    )
    received_peaks, received_totals = (
        lax.all_to_all(prompt_peaks[None], "pre", split_axis=1, concat_axis=0, tiled=True),
        lax.all_to_all(prompt_totals[None], "pre", split_axis=1, concat_axis=0, tiled=True),
    )
    attention = merge_parts(
        jnp.concatenate([received_results, suffix_results[None]], 0),
        jnp.concatenate([received_peaks, suffix_peaks[None]], 0),
        jnp.concatenate([received_totals, suffix_totals[None]], 0),
    )
    head_rows = lax.all_to_all(attention, "pre", split_axis=1, concat_axis=0, tiled=True)
    flat_rows = head_rows.reshape(group_count, head_share * head_width)
    return lax.psum_scatter(
        jnp.dot(flat_rows, out_weight, preferred_element_type=jnp.float32).astype(jnp.bfloat16),
        "pre",
        scatter_dimension=0,
        tiled=True,
    )


MESH = pl.DeviceIdType.MESH
LOG2E = 1.4426950408889634
CUTS = 8


def head_of(samp, pre, key_heads):
    return lax.rem(samp + pre // 2 + 2 * lax.rem(pre, 2), key_heads)


def fused_kernel(
    samp,
    pre,
    length_ref,
    prompt_ref,
    q_ref,
    pk_ref,
    pv_ref,
    sk_ref,
    sv_ref,
    w_ref,
    out_ref,
    qin,
    qf,
    qstage,
    qbuf,
    kvbuf,
    sk,
    sv,
    w,
    sufstage,
    sufbuf,
    ostage,
    obuf,
    sstage,
    sbuf,
    tscr,
    attscr,
    cut,
    rstage,
    rbuf,
    q_send,
    q_recv,
    kv_send,
    kv_recv,
    local_sem,
    suf_send,
    suf_recv,
    o_send,
    o_recv,
    s_send,
    s_recv,
    r_send,
    r_recv,
):
    key_heads = pk_ref.shape[0]
    width = q_ref.shape[2]
    share = pk_ref.shape[1]
    total = samp * pre
    g = lax.axis_index("samp")
    b = lax.axis_index("pre")
    me = g * pre + b
    head = head_of(g, b, key_heads)
    scale = LOG2E / math.sqrt(width)

    def go(source, target, send, recv, to_samp, to_pre):
        pltpu.make_async_remote_copy(
            src_ref=source,
            dst_ref=target,
            send_sem=send,
            recv_sem=recv,
            device_id=(to_samp, to_pre),
            device_id_type=MESH,
        ).start()

    def drain(ref, sem):
        pltpu.make_async_copy(ref, ref, sem).wait()

    pltpu.make_async_copy(q_ref, qin, local_sem.at[3]).start()
    barrier = pltpu.get_barrier_semaphore()

    @pl.loop(1, total)
    def _(i):
        t = lax.rem(me + i, total)
        pl.semaphore_signal(
            barrier, inc=1, device_id=(t // pre, lax.rem(t, pre)), device_id_type=MESH
        )

    pltpu.make_async_copy(sk_ref, sk, local_sem.at[0]).start()
    pltpu.make_async_copy(sv_ref, sv, local_sem.at[1]).start()
    pltpu.make_async_copy(pk_ref.at[head], kvbuf.at[g, 0], kv_recv.at[g]).start()
    pltpu.make_async_copy(pv_ref.at[head], kvbuf.at[g, 1], kv_recv.at[g]).start()
    pltpu.make_async_copy(w_ref, w, local_sem.at[2]).start()

    pltpu.make_async_copy(q_ref, qin, local_sem.at[3]).wait()
    qf[...] = qin[...].astype(jnp.float32)
    for h in range(key_heads):
        for c in range(2):
            for s in range(2):
                row = 16 * h + 8 * c + 4 * s
                tscr[pl.ds(row, 4), :] = qf[s, pl.ds(8 * h + 4 * c, 4), :]
    for h in range(key_heads):
        qstage[h] = tscr[pl.ds(16 * h, 16), :].astype(jnp.bfloat16)

    pltpu.make_async_copy(qstage.at[head], qbuf.at[me], q_recv).start()
    pl.semaphore_wait(barrier, total - 1)

    @pl.loop(1, total)
    def _(i):
        t = lax.rem(me + i, total)
        to_samp, to_pre = t // pre, lax.rem(t, pre)
        go(
            qstage.at[head_of(to_samp, to_pre, key_heads)],
            qbuf.at[me],
            q_send,
            q_recv,
            to_samp,
            to_pre,
        )

    for step in range(1, samp):
        to = lax.rem(g + step, samp)
        his = head_of(to, b, key_heads)
        go(pk_ref.at[his], kvbuf.at[g, 0], kv_send, kv_recv.at[g], to, b)
        go(pv_ref.at[his], kvbuf.at[g, 1], kv_send, kv_recv.at[g], to, b)

    pltpu.make_async_copy(sk_ref, sk, local_sem.at[0]).wait()
    pltpu.make_async_copy(sv_ref, sv, local_sem.at[1]).wait()
    slots = sk.shape[2]
    rows = lax.broadcasted_iota(jnp.int32, (16, 2 * slots), 0)
    cols = lax.broadcasted_iota(jnp.int32, (16, 2 * slots), 1)
    second_row = lax.rem(rows, 8) >= 4
    first_end = jnp.where(second_row, 0, length_ref[0])
    second_end = jnp.where(second_row, length_ref[1], 0) + slots
    seen = cols < jnp.where(cols < slots, first_end, second_end)
    for h in range(key_heads):
        keys = jnp.concatenate([sk[0, h], sk[1, h]], axis=0)
        values = jnp.concatenate([sv[0, h], sv[1, h]], axis=0)
        scores = lax.dot_general(
            qstage[h], keys, (((1,), (1,)), ((), ())), preferred_element_type=jnp.float32
        )
        scores = jnp.where(seen, scores * scale, NEGATIVE)
        peaks = jnp.max(scores, axis=1, keepdims=True)
        weights = jnp.exp2(scores - peaks)
        totals = jnp.sum(weights, axis=1, keepdims=True)
        results = jnp.dot(weights.astype(jnp.bfloat16), values, preferred_element_type=jnp.float32)
        peaks = jnp.broadcast_to(peaks, (16, width))
        totals = jnp.broadcast_to(totals, (16, width))
        for c in range(2):
            sufstage[2 * h + c, 0:8] = results[8 * c : 8 * c + 8]
            sufstage[2 * h + c, 8:16] = peaks[8 * c : 8 * c + 8]
            sufstage[2 * h + c, 16:24] = totals[8 * c : 8 * c + 8]

    pltpu.make_async_copy(sufstage.at[b], sufbuf.at[b], suf_recv).start()

    @pl.loop(1, pre)
    def _(i):
        to = lax.rem(b + i, pre)
        go(sufstage.at[to], sufbuf.at[b], suf_send, suf_recv, g, to)

    drain(qbuf, q_recv)
    queries = qbuf[...].reshape(total * 16, width)
    count = total * 16
    peak = sums = result = None
    for step in range(samp):
        slot = lax.rem(g + step, samp)
        drain(kvbuf.at[slot], kv_recv.at[slot])
        scores = lax.dot_general(
            kvbuf[slot, 0],
            queries,
            (((1,), (1,)), ((), ())),
            preferred_element_type=jnp.float32,
        )
        first = (b * samp + slot) * share
        place = first + lax.broadcasted_iota(jnp.int32, (share, count), 0)
        scores = jnp.where(place < prompt_ref[0], scores * scale, NEGATIVE)
        new_peak = jnp.max(scores, axis=0, keepdims=True)
        if step:
            new_peak = jnp.maximum(new_peak, peak)
        weights = jnp.exp2(scores - new_peak)
        new_sums = jnp.sum(weights, axis=0, keepdims=True)
        new_result = lax.dot_general(
            kvbuf[slot, 1],
            weights.astype(jnp.bfloat16),
            (((0,), (0,)), ((), ())),
            preferred_element_type=jnp.float32,
        )
        if step:
            keep = jnp.exp2(peak - new_peak)
            new_sums = new_sums + keep * sums
            new_result = new_result + keep * result
        peak, sums, result = new_peak, new_sums, new_result

    per = pre * 16
    for t in range(samp):
        block = result[:, per * t : per * (t + 1)].T.reshape(pre, 2, 8, width)
        for c in range(2):
            ostage[t, c] = block[:, c].reshape(pre * 8, width).astype(jnp.bfloat16)
        tile = lax.broadcasted_iota(jnp.int32, (8, per), 0)
        sstage[t] = jnp.where(
            tile == 0, peak[:, per * t : per * (t + 1)], sums[:, per * t : per * (t + 1)]
        )

    slot8 = pl.ds(pl.multiple_of(b * 8, 8), 8)
    for step in range(samp):
        to = lax.rem(g + step, samp)
        for c in range(2):
            k = 2 * head + c

            def here(to=to, c=c):
                pltpu.make_async_copy(ostage.at[to, c], obuf.at[b], o_recv).start()
                pltpu.make_async_copy(sstage.at[to], sbuf.at[slot8], s_recv).start()

            def there(to=to, c=c, k=k):
                go(ostage.at[to, c], obuf.at[b], o_send, o_recv, to, k)
                go(sstage.at[to], sbuf.at[slot8], s_send, s_recv, to, k)

            if step:
                there()
            else:
                pl.when(k == b)(here)
                pl.when(k != b)(there)

    drain(sufbuf, suf_recv)
    suffix = sufbuf[...]
    suffix_result = suffix[:, 0:8].reshape(pre * 8, width)
    suffix_peak = suffix[:, 8:16].reshape(pre * 8, width)
    suffix_total = suffix[:, 16:24].reshape(pre * 8, width)
    drain(sbuf, s_recv)
    peaks = sbuf[pl.ds(0, pre, stride=8), :]
    totals = sbuf[pl.ds(1, pre, stride=8), :]
    top = jnp.max(peaks, axis=0, keepdims=True)
    shares = jnp.exp2(peaks - top)
    bottom = jnp.sum(shares * totals, axis=0, keepdims=True)
    stacked = jnp.concatenate(
        [
            shares,
            jnp.broadcast_to(top, (8, per)),
            jnp.broadcast_to(bottom, (8, per)),
            jnp.zeros((per - 16 - pre, per), jnp.float32),
        ],
        axis=0,
    )
    tscr[...] = stacked.T
    turned = tscr[...].reshape(pre, 2, 8, per)
    turned = jnp.where(lax.rem(b, 2) == 0, turned[:, 0], turned[:, 1]).reshape(pre * 8, per)
    drain(obuf, o_recv)
    prompt_result = jnp.zeros((pre * 8, width), jnp.float32)
    for i in range(pre):
        prompt_result += turned[:, i : i + 1] * obuf[i].astype(jnp.float32)
    prompt_peak = turned[:, pre : pre + 1]
    prompt_total = turned[:, pre + 8 : pre + 9]
    highest = jnp.maximum(prompt_peak, suffix_peak)
    old = jnp.exp2(prompt_peak - highest)
    new = jnp.exp2(suffix_peak - highest)
    attscr[...] = (old * prompt_result + new * suffix_result) / (
        old * prompt_total + new * suffix_total
    )
    attention = jnp.concatenate(
        [attscr[pl.ds(j, 2 * pre, stride=4), :] for j in range(4)], axis=1
    ).astype(jnp.bfloat16)

    pltpu.make_async_copy(w_ref, w, local_sem.at[2]).wait()
    lanes = cut.shape[2]
    piece = cut.shape[0] * lanes
    for p in range(0, CUTS, 2):
        part = jnp.dot(
            attention,
            w[:, p * piece : (p + 2) * piece],
            preferred_element_type=jnp.float32,
        )
        for i in range(2):
            for n in range(cut.shape[0]):
                at = i * piece + n * lanes
                cut[n, pl.ds(p + i, 2 * pre, stride=CUTS), :] = part[:, at : at + lanes]
    for n in range(cut.shape[0]):
        rows = cut[n].reshape(pre, 2 * CUTS, lanes)
        rstage[:, :, n * lanes : (n + 1) * lanes] = rows.astype(jnp.bfloat16)

    pltpu.make_async_copy(rstage.at[b], rbuf.at[b], r_recv).start()

    @pl.loop(1, pre)
    def _(i):
        to = lax.rem(b + i, pre)
        go(rstage.at[to], rbuf.at[b], r_send, r_recv, g, to)

    drain(rbuf, r_recv)
    out_ref[...] = jnp.sum(rbuf[...].astype(jnp.float32), axis=0).astype(jnp.bfloat16)

    drain(qbuf.at[pl.ds(0, total - 1)], q_send)
    drain(kvbuf.at[pl.ds(0, samp - 1)], kv_send)
    drain(sufbuf.at[pl.ds(0, pre - 1)], suf_send)
    drain(rbuf.at[pl.ds(0, pre - 1)], r_send)
    mine = (2 * head == b) | (2 * head + 1 == b)

    @pl.when(mine)
    def _():
        drain(obuf.at[pl.ds(0, pre - 1)], o_send)
        drain(sbuf.at[pl.ds(0, 8 * (pre - 1))], s_send)

    @pl.when(jnp.logical_not(mine))
    def _():
        drain(obuf, o_send)
        drain(sbuf, s_send)


def fused_shards(
    samp,
    pre,
    queries,
    prefix_keys,
    prefix_values,
    suffix_keys,
    suffix_values,
    suffix_lengths,
    prompt_length,
    out_weight,
):
    own, heads, width = queries.shape
    key_heads, share, _ = prefix_keys.shape
    features = out_weight.shape[1]
    piece = features // CUTS
    total = samp * pre
    bf16, f32 = jnp.bfloat16, jnp.float32
    dma = pltpu.SemaphoreType.DMA
    vmem = pl.BlockSpec(memory_space=pltpu.VMEM)
    smem = pl.BlockSpec(memory_space=pltpu.SMEM)
    hbm = pl.BlockSpec(memory_space=pltpu.HBM)
    out = pl.pallas_call(
        functools.partial(fused_kernel, samp, pre),
        out_shape=jax.ShapeDtypeStruct((own * CUTS, piece), bf16),
        in_specs=[smem, smem, hbm, hbm, hbm, hbm, hbm, hbm],
        out_specs=vmem,
        scratch_shapes=[
            pltpu.VMEM(queries.shape, bf16),
            pltpu.VMEM(queries.shape, f32),
            pltpu.VMEM((key_heads, 16, width), bf16),
            pltpu.VMEM((total, 16, width), bf16),
            pltpu.VMEM((samp, 2, share, width), bf16),
            pltpu.VMEM(suffix_keys.shape, bf16),
            pltpu.VMEM(suffix_values.shape, bf16),
            pltpu.VMEM(out_weight.shape, bf16),
            pltpu.VMEM((pre, 24, width), f32),
            pltpu.VMEM((pre, 24, width), f32),
            pltpu.VMEM((samp, 2, pre * 8, width), bf16),
            pltpu.VMEM((pre, pre * 8, width), bf16),
            pltpu.VMEM((samp, 8, pre * 16), f32),
            pltpu.VMEM((pre * 8, pre * 16), f32),
            pltpu.VMEM((pre * 16, width), f32),
            pltpu.VMEM((pre * 8, width), f32),
            pltpu.VMEM((piece // 128, own * pre * CUTS, 128), f32),
            pltpu.VMEM((pre, own * CUTS, piece), bf16),
            pltpu.VMEM((pre, own * CUTS, piece), bf16),
            dma,
            dma,
            dma,
            dma((samp,)),
            dma((4,)),
            dma,
            dma,
            dma,
            dma,
            dma,
            dma,
            dma,
            dma,
        ],
        compiler_params=pltpu.CompilerParams(
            collective_id=0, has_side_effects=True, vmem_limit_bytes=60 * 1024 * 1024
        ),
        cost_estimate=pl.CostEstimate(
            flops=300_000_000, bytes_accessed=7_000_000, transcendentals=400_000
        ),
    )(
        suffix_lengths,
        prompt_length,
        queries,
        prefix_keys,
        prefix_values,
        suffix_keys,
        suffix_values,
        out_weight,
    )
    return out.reshape(own, features)


def solution(mesh):
    samp, pre = mesh.shape["samp"], mesh.shape["pre"]

    def body(queries, prefix_keys, *rest):
        own, heads, width = queries.shape
        key_heads = prefix_keys.shape[0]
        fits = (
            samp == key_heads
            and pre == 2 * key_heads
            and heads == 8 * key_heads
            and own == 2
            and pre * 16 == width
        )
        if fits:
            return fused_shards(samp, pre, queries, prefix_keys, *rest)
        return shards(queries, prefix_keys, *rest)

    return jax.shard_map(
        body,
        mesh=mesh,
        in_specs=(
            P(("samp", "pre"), None, None),
            P(None, ("pre", "samp"), None),
            P(None, ("pre", "samp"), None),
            P(("samp", "pre"), None, None, None),
            P(("samp", "pre"), None, None, None),
            P(("samp", "pre")),
            P(),
            P("pre", None),
        ),
        out_specs=P(("samp", "pre"), None),
        check_vma=False,
    )
```

```python
import functools
import math

import jax
import jax.numpy as jnp
from jax import lax
from jax.experimental import pallas as pl
from jax.experimental.pallas import tpu as pltpu
from jax.sharding import PartitionSpec as P

NEGATIVE = -1e30


def prompt_partial(grouped, block_keys, block_values, visible):
    scaling = 1.0 / math.sqrt(grouped.shape[-1])
    by_head = jnp.transpose(grouped, (1, 0, 2, 3))

    def one_head(operands):
        head_queries, head_keys, head_values = operands
        scores = (
            lax.dot_general(
                head_queries,
                head_keys,
                (((2,), (1,)), ((), ())),
                preferred_element_type=jnp.float32,
            )
            * scaling
        )
        scores = jnp.where(visible, scores, NEGATIVE)
        peaks = jnp.max(scores, axis=-1)
        weights = jnp.where(visible, jnp.exp(scores - peaks[..., None]), 0.0)
        totals = jnp.sum(weights, axis=-1)
        results = lax.dot_general(
            weights.astype(jnp.bfloat16),
            head_values,
            (((2,), (0,)), ((), ())),
            preferred_element_type=jnp.float32,
        )
        return (results.astype(jnp.bfloat16), peaks, totals)

    results, peaks, totals = lax.map(one_head, (by_head, block_keys, block_values))
    count = grouped.shape[0]
    heads = grouped.shape[1] * grouped.shape[2]
    results = jnp.transpose(results, (1, 0, 2, 3)).reshape(count, heads, grouped.shape[3])
    peaks = jnp.transpose(peaks, (1, 0, 2)).reshape(count, heads)
    totals = jnp.transpose(totals, (1, 0, 2)).reshape(count, heads)
    return (results, peaks, totals)


def suffix_partial(grouped, suffix_keys, suffix_values, suffix_lengths):
    scaling = 1.0 / math.sqrt(grouped.shape[-1])
    slots = suffix_keys.shape[2]
    visible = (jnp.arange(slots, dtype=jnp.int32)[None, :] < suffix_lengths[:, None])[
        :, None, None, :
    ]
    scores = (
        jnp.einsum("sgjd,sgpd->sgjp", grouped, suffix_keys, preferred_element_type=jnp.float32)
        * scaling
    )
    scores = jnp.where(visible, scores, NEGATIVE)
    peaks = jnp.max(scores, axis=-1)
    weights = jnp.where(visible, jnp.exp(scores - peaks[..., None]), 0.0)
    totals = jnp.sum(weights, axis=-1)
    results = jnp.einsum(
        "sgjp,sgpd->sgjd",
        weights.astype(jnp.bfloat16),
        suffix_values,
        preferred_element_type=jnp.float32,
    )
    count = grouped.shape[0]
    heads = grouped.shape[1] * grouped.shape[2]
    return (
        results.astype(jnp.bfloat16).reshape(count, heads, grouped.shape[3]),
        peaks.reshape(count, heads),
        totals.reshape(count, heads),
    )


def merge_parts(results, peaks, totals):
    highest = jnp.max(peaks, axis=0)
    weights = jnp.exp(peaks - highest)
    denominator = jnp.sum(weights * totals, axis=0)
    numerator = jnp.sum(weights[..., None] * results.astype(jnp.float32), axis=0)
    return (numerator / denominator[..., None]).astype(jnp.bfloat16)


def shards(
    queries,
    prefix_keys,
    prefix_values,
    suffix_keys,
    suffix_values,
    suffix_lengths,
    prompt_length,
    out_weight,
):
    own_samples = queries.shape[0]
    heads = queries.shape[1]
    head_width = queries.shape[2]
    key_heads = prefix_keys.shape[0]
    ratio = heads // key_heads
    groups = lax.axis_size("pre")
    head_share = heads // groups
    block_keys, block_values = (
        lax.all_gather(prefix_keys, "samp", axis=1, tiled=True),
        lax.all_gather(prefix_values, "samp", axis=1, tiled=True),
    )
    block_length = block_keys.shape[1]
    group_queries = lax.all_gather(queries, "pre", axis=0, tiled=True)
    group_count = group_queries.shape[0]
    positions = lax.axis_index("pre") * block_length + jnp.arange(block_length, dtype=jnp.int32)
    visible = positions < prompt_length[0]
    own_grouped = queries.reshape(own_samples, key_heads, ratio, head_width)
    suffix_results, suffix_peaks, suffix_totals = suffix_partial(
        own_grouped, suffix_keys, suffix_values, suffix_lengths
    )
    group_grouped = group_queries.reshape(group_count, key_heads, ratio, head_width)
    prompt_results, prompt_peaks, prompt_totals = prompt_partial(
        group_grouped, block_keys, block_values, visible
    )
    received_results = lax.all_to_all(
        prompt_results[None], "pre", split_axis=1, concat_axis=0, tiled=True
    )
    received_peaks, received_totals = (
        lax.all_to_all(prompt_peaks[None], "pre", split_axis=1, concat_axis=0, tiled=True),
        lax.all_to_all(prompt_totals[None], "pre", split_axis=1, concat_axis=0, tiled=True),
    )
    attention = merge_parts(
        jnp.concatenate([received_results, suffix_results[None]], 0),
        jnp.concatenate([received_peaks, suffix_peaks[None]], 0),
        jnp.concatenate([received_totals, suffix_totals[None]], 0),
    )
    head_rows = lax.all_to_all(attention, "pre", split_axis=1, concat_axis=0, tiled=True)
    flat_rows = head_rows.reshape(group_count, head_share * head_width)
    return lax.psum_scatter(
        jnp.dot(flat_rows, out_weight, preferred_element_type=jnp.float32).astype(jnp.bfloat16),
        "pre",
        scatter_dimension=0,
        tiled=True,
    )


MESH = pl.DeviceIdType.MESH
LOG2E = 1.4426950408889634
CUTS = 8


def head_of(samp, pre, key_heads):
    return lax.rem(samp + 3 * (pre // 2) + 2 * lax.rem(pre, 2), key_heads)


def fused_kernel(
    samp,
    pre,
    length_ref,
    prompt_ref,
    q_ref,
    pk_ref,
    pv_ref,
    sk_ref,
    sv_ref,
    w_ref,
    out_ref,
    qin,
    qf,
    qstage,
    qbuf,
    kvbuf,
    sk,
    sv,
    w,
    sufstage,
    sufbuf,
    ostage,
    obuf,
    sstage,
    sbuf,
    tscr,
    attscr,
    cut,
    rstage,
    rbuf,
    q_send,
    q_recv,
    kv_send,
    kv_recv,
    local_sem,
    suf_send,
    suf_recv,
    o_send,
    o_recv,
    s_send,
    s_recv,
    r_send,
    r_recv,
):
    key_heads = pk_ref.shape[0]
    width = q_ref.shape[2]
    share = pk_ref.shape[1]
    total = samp * pre
    g = lax.axis_index("samp")
    b = lax.axis_index("pre")
    me = g * pre + b
    head = head_of(g, b, key_heads)
    scale = LOG2E / math.sqrt(width)

    def go(source, target, send, recv, to_samp, to_pre):
        pltpu.make_async_remote_copy(
            src_ref=source,
            dst_ref=target,
            send_sem=send,
            recv_sem=recv,
            device_id=(to_samp, to_pre),
            device_id_type=MESH,
        ).start()

    def drain(ref, sem):
        pltpu.make_async_copy(ref, ref, sem).wait()

    pltpu.make_async_copy(q_ref, qin, local_sem.at[3]).start()
    barrier = pltpu.get_barrier_semaphore()

    @pl.loop(1, total)
    def _(i):
        t = lax.rem(me + i, total)
        pl.semaphore_signal(
            barrier, inc=1, device_id=(t // pre, lax.rem(t, pre)), device_id_type=MESH
        )

    pltpu.make_async_copy(sk_ref, sk, local_sem.at[0]).start()
    pltpu.make_async_copy(sv_ref, sv, local_sem.at[1]).start()
    pltpu.make_async_copy(pk_ref.at[head], kvbuf.at[g, 0], kv_recv.at[g]).start()
    pltpu.make_async_copy(pv_ref.at[head], kvbuf.at[g, 1], kv_recv.at[g]).start()
    pltpu.make_async_copy(w_ref, w, local_sem.at[2]).start()

    pltpu.make_async_copy(q_ref, qin, local_sem.at[3]).wait()
    qf[...] = qin[...].astype(jnp.float32)
    for h in range(key_heads):
        for c in range(2):
            for s in range(2):
                row = 16 * h + 8 * c + 4 * s
                tscr[pl.ds(row, 4), :] = qf[s, pl.ds(8 * h + 4 * c, 4), :]
    for h in range(key_heads):
        qstage[h] = tscr[pl.ds(16 * h, 16), :].astype(jnp.bfloat16)

    pltpu.make_async_copy(qstage.at[head], qbuf.at[me], q_recv).start()
    pl.semaphore_wait(barrier, total - 1)

    @pl.loop(1, total)
    def _(i):
        t = lax.rem(me + i, total)
        to_samp, to_pre = t // pre, lax.rem(t, pre)
        go(
            qstage.at[head_of(to_samp, to_pre, key_heads)],
            qbuf.at[me],
            q_send,
            q_recv,
            to_samp,
            to_pre,
        )

    for step in range(1, samp):
        to = lax.rem(g + step, samp)
        his = head_of(to, b, key_heads)
        go(pk_ref.at[his], kvbuf.at[g, 0], kv_send, kv_recv.at[g], to, b)
        go(pv_ref.at[his], kvbuf.at[g, 1], kv_send, kv_recv.at[g], to, b)

    pltpu.make_async_copy(sk_ref, sk, local_sem.at[0]).wait()
    pltpu.make_async_copy(sv_ref, sv, local_sem.at[1]).wait()
    slots = sk.shape[2]
    rows = lax.broadcasted_iota(jnp.int32, (16, 2 * slots), 0)
    cols = lax.broadcasted_iota(jnp.int32, (16, 2 * slots), 1)
    second_row = lax.rem(rows, 8) >= 4
    first_end = jnp.where(second_row, 0, length_ref[0])
    second_end = jnp.where(second_row, length_ref[1], 0) + slots
    seen = cols < jnp.where(cols < slots, first_end, second_end)
    for h in range(key_heads):
        keys = jnp.concatenate([sk[0, h], sk[1, h]], axis=0)
        values = jnp.concatenate([sv[0, h], sv[1, h]], axis=0)
        scores = lax.dot_general(
            qstage[h], keys, (((1,), (1,)), ((), ())), preferred_element_type=jnp.float32
        )
        scores = jnp.where(seen, scores * scale, NEGATIVE)
        peaks = jnp.max(scores, axis=1, keepdims=True)
        weights = jnp.exp2(scores - peaks)
        totals = jnp.sum(weights, axis=1, keepdims=True)
        results = jnp.dot(weights.astype(jnp.bfloat16), values, preferred_element_type=jnp.float32)
        peaks = jnp.broadcast_to(peaks, (16, width))
        totals = jnp.broadcast_to(totals, (16, width))
        for c in range(2):
            sufstage[2 * h + c, 0:8] = results[8 * c : 8 * c + 8]
            sufstage[2 * h + c, 8:16] = peaks[8 * c : 8 * c + 8]
            sufstage[2 * h + c, 16:24] = totals[8 * c : 8 * c + 8]

    pltpu.make_async_copy(sufstage.at[b], sufbuf.at[b], suf_recv).start()

    @pl.loop(1, pre)
    def _(i):
        to = lax.rem(b + i, pre)
        go(sufstage.at[to], sufbuf.at[b], suf_send, suf_recv, g, to)

    drain(qbuf, q_recv)
    queries = qbuf[...].reshape(total * 16, width)
    count = total * 16
    peak = sums = result = None
    for step in range(samp):
        slot = lax.rem(g + step, samp)
        drain(kvbuf.at[slot], kv_recv.at[slot])
        scores = lax.dot_general(
            kvbuf[slot, 0],
            queries,
            (((1,), (1,)), ((), ())),
            preferred_element_type=jnp.float32,
        )
        first = (b * samp + slot) * share
        place = first + lax.broadcasted_iota(jnp.int32, (share, count), 0)
        scores = jnp.where(place < prompt_ref[0], scores * scale, NEGATIVE)
        new_peak = jnp.max(scores, axis=0, keepdims=True)
        if step:
            new_peak = jnp.maximum(new_peak, peak)
        weights = jnp.exp2(scores - new_peak)
        new_sums = jnp.sum(weights, axis=0, keepdims=True)
        new_result = lax.dot_general(
            kvbuf[slot, 1],
            weights.astype(jnp.bfloat16),
            (((0,), (0,)), ((), ())),
            preferred_element_type=jnp.float32,
        )
        if step:
            keep = jnp.exp2(peak - new_peak)
            new_sums = new_sums + keep * sums
            new_result = new_result + keep * result
        peak, sums, result = new_peak, new_sums, new_result

    per = pre * 16
    for t in range(samp):
        block = result[:, per * t : per * (t + 1)].T.reshape(pre, 2, 8, width)
        for c in range(2):
            ostage[t, c] = block[:, c].reshape(pre * 8, width).astype(jnp.bfloat16)
        tile = lax.broadcasted_iota(jnp.int32, (8, per), 0)
        sstage[t] = jnp.where(
            tile == 0, peak[:, per * t : per * (t + 1)], sums[:, per * t : per * (t + 1)]
        )

    slot8 = pl.ds(pl.multiple_of(b * 8, 8), 8)
    for step in range(samp):
        to = lax.rem(g + step, samp)
        for c in range(2):
            k = 2 * head + c

            def here(to=to, c=c):
                pltpu.make_async_copy(ostage.at[to, c], obuf.at[b], o_recv).start()
                pltpu.make_async_copy(sstage.at[to], sbuf.at[slot8], s_recv).start()

            def there(to=to, c=c, k=k):
                go(ostage.at[to, c], obuf.at[b], o_send, o_recv, to, k)
                go(sstage.at[to], sbuf.at[slot8], s_send, s_recv, to, k)

            if step:
                there()
            else:
                pl.when(k == b)(here)
                pl.when(k != b)(there)

    drain(sufbuf, suf_recv)
    suffix = sufbuf[...]
    suffix_result = suffix[:, 0:8].reshape(pre * 8, width)
    suffix_peak = suffix[:, 8:16].reshape(pre * 8, width)
    suffix_total = suffix[:, 16:24].reshape(pre * 8, width)
    drain(sbuf, s_recv)
    peaks = sbuf[pl.ds(0, pre, stride=8), :]
    totals = sbuf[pl.ds(1, pre, stride=8), :]
    top = jnp.max(peaks, axis=0, keepdims=True)
    shares = jnp.exp2(peaks - top)
    bottom = jnp.sum(shares * totals, axis=0, keepdims=True)
    stacked = jnp.concatenate(
        [
            shares,
            jnp.broadcast_to(top, (8, per)),
            jnp.broadcast_to(bottom, (8, per)),
            jnp.zeros((per - 16 - pre, per), jnp.float32),
        ],
        axis=0,
    )
    tscr[...] = stacked.T
    turned = tscr[...].reshape(pre, 2, 8, per)
    turned = jnp.where(lax.rem(b, 2) == 0, turned[:, 0], turned[:, 1]).reshape(pre * 8, per)
    drain(obuf, o_recv)
    prompt_result = jnp.zeros((pre * 8, width), jnp.float32)
    for i in range(pre):
        prompt_result += turned[:, i : i + 1] * obuf[i].astype(jnp.float32)
    prompt_peak = turned[:, pre : pre + 1]
    prompt_total = turned[:, pre + 8 : pre + 9]
    highest = jnp.maximum(prompt_peak, suffix_peak)
    old = jnp.exp2(prompt_peak - highest)
    new = jnp.exp2(suffix_peak - highest)
    attscr[...] = (old * prompt_result + new * suffix_result) / (
        old * prompt_total + new * suffix_total
    )
    attention = jnp.concatenate(
        [attscr[pl.ds(j, 2 * pre, stride=4), :] for j in range(4)], axis=1
    ).astype(jnp.bfloat16)

    pltpu.make_async_copy(w_ref, w, local_sem.at[2]).wait()
    lanes = cut.shape[2]
    piece = cut.shape[0] * lanes
    for p in range(0, CUTS, 2):
        part = jnp.dot(
            attention,
            w[:, p * piece : (p + 2) * piece],
            preferred_element_type=jnp.float32,
        )
        for i in range(2):
            for n in range(cut.shape[0]):
                at = i * piece + n * lanes
                cut[n, pl.ds(p + i, 2 * pre, stride=CUTS), :] = part[:, at : at + lanes]
    for n in range(cut.shape[0]):
        rows = cut[n].reshape(pre, 2 * CUTS, lanes)
        rstage[:, :, n * lanes : (n + 1) * lanes] = rows.astype(jnp.bfloat16)

    pltpu.make_async_copy(rstage.at[b], rbuf.at[b], r_recv).start()

    @pl.loop(1, pre)
    def _(i):
        to = lax.rem(b + i, pre)
        go(rstage.at[to], rbuf.at[b], r_send, r_recv, g, to)

    drain(rbuf, r_recv)
    out_ref[...] = jnp.sum(rbuf[...].astype(jnp.float32), axis=0).astype(jnp.bfloat16)

    drain(qbuf.at[pl.ds(0, total - 1)], q_send)
    drain(kvbuf.at[pl.ds(0, samp - 1)], kv_send)
    drain(sufbuf.at[pl.ds(0, pre - 1)], suf_send)
    drain(rbuf.at[pl.ds(0, pre - 1)], r_send)
    mine = (2 * head == b) | (2 * head + 1 == b)

    @pl.when(mine)
    def _():
        drain(obuf.at[pl.ds(0, pre - 1)], o_send)
        drain(sbuf.at[pl.ds(0, 8 * (pre - 1))], s_send)

    @pl.when(jnp.logical_not(mine))
    def _():
        drain(obuf, o_send)
        drain(sbuf, s_send)


def fused_shards(
    samp,
    pre,
    queries,
    prefix_keys,
    prefix_values,
    suffix_keys,
    suffix_values,
    suffix_lengths,
    prompt_length,
    out_weight,
):
    own, heads, width = queries.shape
    key_heads, share, _ = prefix_keys.shape
    features = out_weight.shape[1]
    piece = features // CUTS
    total = samp * pre
    bf16, f32 = jnp.bfloat16, jnp.float32
    dma = pltpu.SemaphoreType.DMA
    vmem = pl.BlockSpec(memory_space=pltpu.VMEM)
    smem = pl.BlockSpec(memory_space=pltpu.SMEM)
    hbm = pl.BlockSpec(memory_space=pltpu.HBM)
    out = pl.pallas_call(
        functools.partial(fused_kernel, samp, pre),
        out_shape=jax.ShapeDtypeStruct((own * CUTS, piece), bf16),
        in_specs=[smem, smem, hbm, hbm, hbm, hbm, hbm, hbm],
        out_specs=vmem,
        scratch_shapes=[
            pltpu.VMEM(queries.shape, bf16),
            pltpu.VMEM(queries.shape, f32),
            pltpu.VMEM((key_heads, 16, width), bf16),
            pltpu.VMEM((total, 16, width), bf16),
            pltpu.VMEM((samp, 2, share, width), bf16),
            pltpu.VMEM(suffix_keys.shape, bf16),
            pltpu.VMEM(suffix_values.shape, bf16),
            pltpu.VMEM(out_weight.shape, bf16),
            pltpu.VMEM((pre, 24, width), f32),
            pltpu.VMEM((pre, 24, width), f32),
            pltpu.VMEM((samp, 2, pre * 8, width), bf16),
            pltpu.VMEM((pre, pre * 8, width), bf16),
            pltpu.VMEM((samp, 8, pre * 16), f32),
            pltpu.VMEM((pre * 8, pre * 16), f32),
            pltpu.VMEM((pre * 16, width), f32),
            pltpu.VMEM((pre * 8, width), f32),
            pltpu.VMEM((piece // 128, own * pre * CUTS, 128), f32),
            pltpu.VMEM((pre, own * CUTS, piece), bf16),
            pltpu.VMEM((pre, own * CUTS, piece), bf16),
            dma,
            dma,
            dma,
            dma((samp,)),
            dma((4,)),
            dma,
            dma,
            dma,
            dma,
            dma,
            dma,
            dma,
            dma,
        ],
        compiler_params=pltpu.CompilerParams(
            collective_id=0, has_side_effects=True, vmem_limit_bytes=60 * 1024 * 1024
        ),
        cost_estimate=pl.CostEstimate(
            flops=300_000_000, bytes_accessed=7_000_000, transcendentals=400_000
        ),
    )(
        suffix_lengths,
        prompt_length,
        queries,
        prefix_keys,
        prefix_values,
        suffix_keys,
        suffix_values,
        out_weight,
    )
    return out.reshape(own, features)


def solution(mesh):
    samp, pre = mesh.shape["samp"], mesh.shape["pre"]

    def body(queries, prefix_keys, *rest):
        own, heads, width = queries.shape
        key_heads = prefix_keys.shape[0]
        fits = (
            samp == key_heads
            and pre == 2 * key_heads
            and heads == 8 * key_heads
            and own == 2
            and pre * 16 == width
        )
        if fits:
            return fused_shards(samp, pre, queries, prefix_keys, *rest)
        return shards(queries, prefix_keys, *rest)

    return jax.shard_map(
        body,
        mesh=mesh,
        in_specs=(
            P(("samp", "pre"), None, None),
            P(None, ("pre", "samp"), None),
            P(None, ("pre", "samp"), None),
            P(("samp", "pre"), None, None, None),
            P(("samp", "pre"), None, None, None),
            P(("samp", "pre")),
            P(),
            P("pre", None),
        ),
        out_specs=P(("samp", "pre"), None),
        check_vma=False,
    )
```

```python
import functools
import math

import jax
import jax.numpy as jnp
from jax import lax
from jax.experimental import pallas as pl
from jax.experimental.pallas import tpu as pltpu
from jax.sharding import PartitionSpec as P

NEGATIVE = -1e30


def prompt_partial(grouped, block_keys, block_values, visible):
    scaling = 1.0 / math.sqrt(grouped.shape[-1])
    by_head = jnp.transpose(grouped, (1, 0, 2, 3))

    def one_head(operands):
        head_queries, head_keys, head_values = operands
        scores = (
            lax.dot_general(
                head_queries,
                head_keys,
                (((2,), (1,)), ((), ())),
                preferred_element_type=jnp.float32,
            )
            * scaling
        )
        scores = jnp.where(visible, scores, NEGATIVE)
        peaks = jnp.max(scores, axis=-1)
        weights = jnp.where(visible, jnp.exp(scores - peaks[..., None]), 0.0)
        totals = jnp.sum(weights, axis=-1)
        results = lax.dot_general(
            weights.astype(jnp.bfloat16),
            head_values,
            (((2,), (0,)), ((), ())),
            preferred_element_type=jnp.float32,
        )
        return (results.astype(jnp.bfloat16), peaks, totals)

    results, peaks, totals = lax.map(one_head, (by_head, block_keys, block_values))
    count = grouped.shape[0]
    heads = grouped.shape[1] * grouped.shape[2]
    results = jnp.transpose(results, (1, 0, 2, 3)).reshape(count, heads, grouped.shape[3])
    peaks = jnp.transpose(peaks, (1, 0, 2)).reshape(count, heads)
    totals = jnp.transpose(totals, (1, 0, 2)).reshape(count, heads)
    return (results, peaks, totals)


def suffix_partial(grouped, suffix_keys, suffix_values, suffix_lengths):
    scaling = 1.0 / math.sqrt(grouped.shape[-1])
    slots = suffix_keys.shape[2]
    visible = (jnp.arange(slots, dtype=jnp.int32)[None, :] < suffix_lengths[:, None])[
        :, None, None, :
    ]
    scores = (
        jnp.einsum("sgjd,sgpd->sgjp", grouped, suffix_keys, preferred_element_type=jnp.float32)
        * scaling
    )
    scores = jnp.where(visible, scores, NEGATIVE)
    peaks = jnp.max(scores, axis=-1)
    weights = jnp.where(visible, jnp.exp(scores - peaks[..., None]), 0.0)
    totals = jnp.sum(weights, axis=-1)
    results = jnp.einsum(
        "sgjp,sgpd->sgjd",
        weights.astype(jnp.bfloat16),
        suffix_values,
        preferred_element_type=jnp.float32,
    )
    count = grouped.shape[0]
    heads = grouped.shape[1] * grouped.shape[2]
    return (
        results.astype(jnp.bfloat16).reshape(count, heads, grouped.shape[3]),
        peaks.reshape(count, heads),
        totals.reshape(count, heads),
    )


def merge_parts(results, peaks, totals):
    highest = jnp.max(peaks, axis=0)
    weights = jnp.exp(peaks - highest)
    denominator = jnp.sum(weights * totals, axis=0)
    numerator = jnp.sum(weights[..., None] * results.astype(jnp.float32), axis=0)
    return (numerator / denominator[..., None]).astype(jnp.bfloat16)


def shards(
    queries,
    prefix_keys,
    prefix_values,
    suffix_keys,
    suffix_values,
    suffix_lengths,
    prompt_length,
    out_weight,
):
    own_samples = queries.shape[0]
    heads = queries.shape[1]
    head_width = queries.shape[2]
    key_heads = prefix_keys.shape[0]
    ratio = heads // key_heads
    groups = lax.axis_size("pre")
    head_share = heads // groups
    block_keys, block_values = (
        lax.all_gather(prefix_keys, "samp", axis=1, tiled=True),
        lax.all_gather(prefix_values, "samp", axis=1, tiled=True),
    )
    block_length = block_keys.shape[1]
    group_queries = lax.all_gather(queries, "pre", axis=0, tiled=True)
    group_count = group_queries.shape[0]
    positions = lax.axis_index("pre") * block_length + jnp.arange(block_length, dtype=jnp.int32)
    visible = positions < prompt_length[0]
    own_grouped = queries.reshape(own_samples, key_heads, ratio, head_width)
    suffix_results, suffix_peaks, suffix_totals = suffix_partial(
        own_grouped, suffix_keys, suffix_values, suffix_lengths
    )
    group_grouped = group_queries.reshape(group_count, key_heads, ratio, head_width)
    prompt_results, prompt_peaks, prompt_totals = prompt_partial(
        group_grouped, block_keys, block_values, visible
    )
    received_results = lax.all_to_all(
        prompt_results[None], "pre", split_axis=1, concat_axis=0, tiled=True
    )
    received_peaks, received_totals = (
        lax.all_to_all(prompt_peaks[None], "pre", split_axis=1, concat_axis=0, tiled=True),
        lax.all_to_all(prompt_totals[None], "pre", split_axis=1, concat_axis=0, tiled=True),
    )
    attention = merge_parts(
        jnp.concatenate([received_results, suffix_results[None]], 0),
        jnp.concatenate([received_peaks, suffix_peaks[None]], 0),
        jnp.concatenate([received_totals, suffix_totals[None]], 0),
    )
    head_rows = lax.all_to_all(attention, "pre", split_axis=1, concat_axis=0, tiled=True)
    flat_rows = head_rows.reshape(group_count, head_share * head_width)
    return lax.psum_scatter(
        jnp.dot(flat_rows, out_weight, preferred_element_type=jnp.float32).astype(jnp.bfloat16),
        "pre",
        scatter_dimension=0,
        tiled=True,
    )


MESH = pl.DeviceIdType.MESH
LOG2E = 1.4426950408889634
CUTS = 8


def head_of(samp, pre, key_heads):
    return lax.rem(samp // 2 + pre // 4 + lax.rem(pre, 2), 2) * 2 + lax.rem(lax.rem(samp, 2) + pre // 2, 2)


def fused_kernel(
    samp,
    pre,
    length_ref,
    prompt_ref,
    q_ref,
    pk_ref,
    pv_ref,
    sk_ref,
    sv_ref,
    w_ref,
    out_ref,
    qin,
    qf,
    qstage,
    qbuf,
    kvbuf,
    sk,
    sv,
    w,
    sufstage,
    sufbuf,
    ostage,
    obuf,
    sstage,
    sbuf,
    tscr,
    attscr,
    cut,
    rstage,
    rbuf,
    q_send,
    q_recv,
    kv_send,
    kv_recv,
    local_sem,
    suf_send,
    suf_recv,
    o_send,
    o_recv,
    s_send,
    s_recv,
    r_send,
    r_recv,
):
    key_heads = pk_ref.shape[0]
    width = q_ref.shape[2]
    share = pk_ref.shape[1]
    total = samp * pre
    g = lax.axis_index("samp")
    b = lax.axis_index("pre")
    me = g * pre + b
    head = head_of(g, b, key_heads)
    scale = LOG2E / math.sqrt(width)

    def go(source, target, send, recv, to_samp, to_pre):
        pltpu.make_async_remote_copy(
            src_ref=source,
            dst_ref=target,
            send_sem=send,
            recv_sem=recv,
            device_id=(to_samp, to_pre),
            device_id_type=MESH,
        ).start()

    def drain(ref, sem):
        pltpu.make_async_copy(ref, ref, sem).wait()

    pltpu.make_async_copy(q_ref, qin, local_sem.at[3]).start()
    barrier = pltpu.get_barrier_semaphore()

    @pl.loop(1, total)
    def _(i):
        t = lax.rem(me + i, total)
        pl.semaphore_signal(
            barrier, inc=1, device_id=(t // pre, lax.rem(t, pre)), device_id_type=MESH
        )

    pltpu.make_async_copy(sk_ref, sk, local_sem.at[0]).start()
    pltpu.make_async_copy(sv_ref, sv, local_sem.at[1]).start()
    pltpu.make_async_copy(pk_ref.at[head], kvbuf.at[g, 0], kv_recv.at[g]).start()
    pltpu.make_async_copy(pv_ref.at[head], kvbuf.at[g, 1], kv_recv.at[g]).start()
    pltpu.make_async_copy(w_ref, w, local_sem.at[2]).start()

    pltpu.make_async_copy(q_ref, qin, local_sem.at[3]).wait()
    qf[...] = qin[...].astype(jnp.float32)
    for h in range(key_heads):
        for c in range(2):
            for s in range(2):
                row = 16 * h + 8 * c + 4 * s
                tscr[pl.ds(row, 4), :] = qf[s, pl.ds(8 * h + 4 * c, 4), :]
    for h in range(key_heads):
        qstage[h] = tscr[pl.ds(16 * h, 16), :].astype(jnp.bfloat16)

    pltpu.make_async_copy(qstage.at[head], qbuf.at[me], q_recv).start()
    pl.semaphore_wait(barrier, total - 1)

    @pl.loop(1, total)
    def _(i):
        t = lax.rem(me + i, total)
        to_samp, to_pre = t // pre, lax.rem(t, pre)
        go(
            qstage.at[head_of(to_samp, to_pre, key_heads)],
            qbuf.at[me],
            q_send,
            q_recv,
            to_samp,
            to_pre,
        )

    for step in range(1, samp):
        to = lax.rem(g + step, samp)
        his = head_of(to, b, key_heads)
        go(pk_ref.at[his], kvbuf.at[g, 0], kv_send, kv_recv.at[g], to, b)
        go(pv_ref.at[his], kvbuf.at[g, 1], kv_send, kv_recv.at[g], to, b)

    pltpu.make_async_copy(sk_ref, sk, local_sem.at[0]).wait()
    pltpu.make_async_copy(sv_ref, sv, local_sem.at[1]).wait()
    slots = sk.shape[2]
    rows = lax.broadcasted_iota(jnp.int32, (16, 2 * slots), 0)
    cols = lax.broadcasted_iota(jnp.int32, (16, 2 * slots), 1)
    second_row = lax.rem(rows, 8) >= 4
    first_end = jnp.where(second_row, 0, length_ref[0])
    second_end = jnp.where(second_row, length_ref[1], 0) + slots
    seen = cols < jnp.where(cols < slots, first_end, second_end)
    for h in range(key_heads):
        keys = jnp.concatenate([sk[0, h], sk[1, h]], axis=0)
        values = jnp.concatenate([sv[0, h], sv[1, h]], axis=0)
        scores = lax.dot_general(
            qstage[h], keys, (((1,), (1,)), ((), ())), preferred_element_type=jnp.float32
        )
        scores = jnp.where(seen, scores * scale, NEGATIVE)
        peaks = jnp.max(scores, axis=1, keepdims=True)
        weights = jnp.exp2(scores - peaks)
        totals = jnp.sum(weights, axis=1, keepdims=True)
        results = jnp.dot(weights.astype(jnp.bfloat16), values, preferred_element_type=jnp.float32)
        peaks = jnp.broadcast_to(peaks, (16, width))
        totals = jnp.broadcast_to(totals, (16, width))
        for c in range(2):
            sufstage[2 * h + c, 0:8] = results[8 * c : 8 * c + 8]
            sufstage[2 * h + c, 8:16] = peaks[8 * c : 8 * c + 8]
            sufstage[2 * h + c, 16:24] = totals[8 * c : 8 * c + 8]

    pltpu.make_async_copy(sufstage.at[b], sufbuf.at[b], suf_recv).start()

    @pl.loop(1, pre)
    def _(i):
        to = lax.rem(b + i, pre)
        go(sufstage.at[to], sufbuf.at[b], suf_send, suf_recv, g, to)

    drain(qbuf, q_recv)
    queries = qbuf[...].reshape(total * 16, width)
    count = total * 16
    peak = sums = result = None
    for step in range(samp):
        slot = lax.rem(g + step, samp)
        drain(kvbuf.at[slot], kv_recv.at[slot])
        scores = lax.dot_general(
            kvbuf[slot, 0],
            queries,
            (((1,), (1,)), ((), ())),
            preferred_element_type=jnp.float32,
        )
        first = (b * samp + slot) * share
        place = first + lax.broadcasted_iota(jnp.int32, (share, count), 0)
        scores = jnp.where(place < prompt_ref[0], scores * scale, NEGATIVE)
        new_peak = jnp.max(scores, axis=0, keepdims=True)
        if step:
            new_peak = jnp.maximum(new_peak, peak)
        weights = jnp.exp2(scores - new_peak)
        new_sums = jnp.sum(weights, axis=0, keepdims=True)
        new_result = lax.dot_general(
            kvbuf[slot, 1],
            weights.astype(jnp.bfloat16),
            (((0,), (0,)), ((), ())),
            preferred_element_type=jnp.float32,
        )
        if step:
            keep = jnp.exp2(peak - new_peak)
            new_sums = new_sums + keep * sums
            new_result = new_result + keep * result
        peak, sums, result = new_peak, new_sums, new_result

    per = pre * 16
    for t in range(samp):
        block = result[:, per * t : per * (t + 1)].T.reshape(pre, 2, 8, width)
        for c in range(2):
            ostage[t, c] = block[:, c].reshape(pre * 8, width).astype(jnp.bfloat16)
        tile = lax.broadcasted_iota(jnp.int32, (8, per), 0)
        sstage[t] = jnp.where(
            tile == 0, peak[:, per * t : per * (t + 1)], sums[:, per * t : per * (t + 1)]
        )

    slot8 = pl.ds(pl.multiple_of(b * 8, 8), 8)
    for step in (*range(1, samp), 0):
        to = lax.rem(g + step, samp)
        for c in range(2):
            k = 2 * head + c

            def here(to=to, c=c):
                pltpu.make_async_copy(ostage.at[to, c], obuf.at[b], o_recv).start()
                pltpu.make_async_copy(sstage.at[to], sbuf.at[slot8], s_recv).start()

            def there(to=to, c=c, k=k):
                go(ostage.at[to, c], obuf.at[b], o_send, o_recv, to, k)
                go(sstage.at[to], sbuf.at[slot8], s_send, s_recv, to, k)

            if step:
                there()
            else:
                pl.when(k == b)(here)
                pl.when(k != b)(there)

    drain(sufbuf, suf_recv)
    suffix = sufbuf[...]
    suffix_result = suffix[:, 0:8].reshape(pre * 8, width)
    suffix_peak = suffix[:, 8:16].reshape(pre * 8, width)
    suffix_total = suffix[:, 16:24].reshape(pre * 8, width)
    drain(sbuf, s_recv)
    peaks = sbuf[pl.ds(0, pre, stride=8), :]
    totals = sbuf[pl.ds(1, pre, stride=8), :]
    top = jnp.max(peaks, axis=0, keepdims=True)
    shares = jnp.exp2(peaks - top)
    bottom = jnp.sum(shares * totals, axis=0, keepdims=True)
    stacked = jnp.concatenate(
        [
            shares,
            jnp.broadcast_to(top, (8, per)),
            jnp.broadcast_to(bottom, (8, per)),
            jnp.zeros((per - 16 - pre, per), jnp.float32),
        ],
        axis=0,
    )
    tscr[...] = stacked.T
    turned = tscr[...].reshape(pre, 2, 8, per)
    turned = jnp.where(lax.rem(b, 2) == 0, turned[:, 0], turned[:, 1]).reshape(pre * 8, per)
    drain(obuf, o_recv)
    prompt_result = jnp.zeros((pre * 8, width), jnp.float32)
    for i in range(pre):
        prompt_result += turned[:, i : i + 1] * obuf[i].astype(jnp.float32)
    prompt_peak = turned[:, pre : pre + 1]
    prompt_total = turned[:, pre + 8 : pre + 9]
    highest = jnp.maximum(prompt_peak, suffix_peak)
    old = jnp.exp2(prompt_peak - highest)
    new = jnp.exp2(suffix_peak - highest)
    attscr[...] = (old * prompt_result + new * suffix_result) / (
        old * prompt_total + new * suffix_total
    )
    attention = jnp.concatenate(
        [attscr[pl.ds(j, 2 * pre, stride=4), :] for j in range(4)], axis=1
    ).astype(jnp.bfloat16)

    pltpu.make_async_copy(w_ref, w, local_sem.at[2]).wait()
    lanes = cut.shape[2]
    piece = cut.shape[0] * lanes
    for p in range(0, CUTS, 2):
        part = jnp.dot(
            attention,
            w[:, p * piece : (p + 2) * piece],
            preferred_element_type=jnp.float32,
        )
        for i in range(2):
            for n in range(cut.shape[0]):
                at = i * piece + n * lanes
                cut[n, pl.ds(p + i, 2 * pre, stride=CUTS), :] = part[:, at : at + lanes]
    for n in range(cut.shape[0]):
        rows = cut[n].reshape(pre, 2 * CUTS, lanes)
        rstage[:, :, n * lanes : (n + 1) * lanes] = rows.astype(jnp.bfloat16)

    pltpu.make_async_copy(rstage.at[b], rbuf.at[b], r_recv).start()

    @pl.loop(1, pre)
    def _(i):
        to = lax.rem(b + i, pre)
        go(rstage.at[to], rbuf.at[b], r_send, r_recv, g, to)

    drain(rbuf, r_recv)
    out_ref[...] = jnp.sum(rbuf[...].astype(jnp.float32), axis=0).astype(jnp.bfloat16)

    drain(qbuf.at[pl.ds(0, total - 1)], q_send)
    drain(kvbuf.at[pl.ds(0, samp - 1)], kv_send)
    drain(sufbuf.at[pl.ds(0, pre - 1)], suf_send)
    drain(rbuf.at[pl.ds(0, pre - 1)], r_send)
    mine = (2 * head == b) | (2 * head + 1 == b)

    @pl.when(mine)
    def _():
        drain(obuf.at[pl.ds(0, pre - 1)], o_send)
        drain(sbuf.at[pl.ds(0, 8 * (pre - 1))], s_send)

    @pl.when(jnp.logical_not(mine))
    def _():
        drain(obuf, o_send)
        drain(sbuf, s_send)


def fused_shards(
    samp,
    pre,
    queries,
    prefix_keys,
    prefix_values,
    suffix_keys,
    suffix_values,
    suffix_lengths,
    prompt_length,
    out_weight,
):
    own, heads, width = queries.shape
    key_heads, share, _ = prefix_keys.shape
    features = out_weight.shape[1]
    piece = features // CUTS
    total = samp * pre
    bf16, f32 = jnp.bfloat16, jnp.float32
    dma = pltpu.SemaphoreType.DMA
    vmem = pl.BlockSpec(memory_space=pltpu.VMEM)
    smem = pl.BlockSpec(memory_space=pltpu.SMEM)
    hbm = pl.BlockSpec(memory_space=pltpu.HBM)
    out = pl.pallas_call(
        functools.partial(fused_kernel, samp, pre),
        out_shape=jax.ShapeDtypeStruct((own * CUTS, piece), bf16),
        in_specs=[smem, smem, hbm, hbm, hbm, hbm, hbm, hbm],
        out_specs=vmem,
        scratch_shapes=[
            pltpu.VMEM(queries.shape, bf16),
            pltpu.VMEM(queries.shape, f32),
            pltpu.VMEM((key_heads, 16, width), bf16),
            pltpu.VMEM((total, 16, width), bf16),
            pltpu.VMEM((samp, 2, share, width), bf16),
            pltpu.VMEM(suffix_keys.shape, bf16),
            pltpu.VMEM(suffix_values.shape, bf16),
            pltpu.VMEM(out_weight.shape, bf16),
            pltpu.VMEM((pre, 24, width), f32),
            pltpu.VMEM((pre, 24, width), f32),
            pltpu.VMEM((samp, 2, pre * 8, width), bf16),
            pltpu.VMEM((pre, pre * 8, width), bf16),
            pltpu.VMEM((samp, 8, pre * 16), f32),
            pltpu.VMEM((pre * 8, pre * 16), f32),
            pltpu.VMEM((pre * 16, width), f32),
            pltpu.VMEM((pre * 8, width), f32),
            pltpu.VMEM((piece // 128, own * pre * CUTS, 128), f32),
            pltpu.VMEM((pre, own * CUTS, piece), bf16),
            pltpu.VMEM((pre, own * CUTS, piece), bf16),
            dma,
            dma,
            dma,
            dma((samp,)),
            dma((4,)),
            dma,
            dma,
            dma,
            dma,
            dma,
            dma,
            dma,
            dma,
        ],
        compiler_params=pltpu.CompilerParams(
            collective_id=0, has_side_effects=True, vmem_limit_bytes=60 * 1024 * 1024
        ),
        cost_estimate=pl.CostEstimate(
            flops=300_000_000, bytes_accessed=7_000_000, transcendentals=400_000
        ),
    )(
        suffix_lengths,
        prompt_length,
        queries,
        prefix_keys,
        prefix_values,
        suffix_keys,
        suffix_values,
        out_weight,
    )
    return out.reshape(own, features)


def solution(mesh):
    samp, pre = mesh.shape["samp"], mesh.shape["pre"]

    def body(queries, prefix_keys, *rest):
        own, heads, width = queries.shape
        key_heads = prefix_keys.shape[0]
        fits = (
            samp == key_heads
            and pre == 2 * key_heads
            and heads == 8 * key_heads
            and own == 2
            and pre * 16 == width
        )
        if fits:
            return fused_shards(samp, pre, queries, prefix_keys, *rest)
        return shards(queries, prefix_keys, *rest)

    return jax.shard_map(
        body,
        mesh=mesh,
        in_specs=(
            P(("samp", "pre"), None, None),
            P(None, ("pre", "samp"), None),
            P(None, ("pre", "samp"), None),
            P(("samp", "pre"), None, None, None),
            P(("samp", "pre"), None, None, None),
            P(("samp", "pre")),
            P(),
            P("pre", None),
        ),
        out_specs=P(("samp", "pre"), None),
        check_vma=False,
    )
```
